32 devices in a mesh: sta: 8 (over y, x, core), tm: 4 (over z).
Axes of the slice: x: 2, y: 2, z: 4, core: 2. Of those that a mesh axis runs over, the one named last changes fastest.
Arguments:
- spectra: bfloat16 [8, 1024, 2, 4096], P('tm', None, None, 'sta')
- src_ids: int32 [3, 8], replicated, may hold values from 0 to 1023, as said below
Outputs:
- correlations: float32 [3, 256, 8, 1024], P(None, 'tm', None, 'sta')
The draws below stay inside these ranges and needn't reach their ends.
Inputs may be any that keep to these rules, and one draw needn't show every extreme that they name: `src_ids`: the 8 ids of a round are distinct and all lie in one block of 128 consecutive stations that starts at a multiple of 128.
All inputs are finite; a program needn't handle non-finite values.
Results may differ from the reference program's by a relative error of at most 0.0056.
Values may be sent and summed in bfloat16 or wider, within the bound.
A program may use at most 128 MiB of HBM per device.

```python
import math
import jax
import jax.numpy as jnp
from jax import lax

STA_DEV = 128
HR_DEV = 2
BINS = 4096
BLOCK = 64
LAGS = 256
NSRC = 8
ROUNDS = 3
STATIONS = 1024
HOURS = 8


def draw_spectra(key, part):
    key_base, key_row, key_block = jax.random.split(jax.random.fold_in(key, 11), 3)
    block_num = BINS // BLOCK
    full = (HOURS, STATIONS, 2, block_num, BLOCK)
    base = jnp.clip(jax.random.normal(key_base, full, jnp.float32), -6.0, 6.0)
    row_scale = jnp.exp(jax.random.uniform(key_row, (HOURS, STATIONS, 1, 1, 1), jnp.float32, 0.0, math.log(10.0)))
    block_scale = jnp.exp(jax.random.uniform(key_block, (HOURS, STATIONS, 1, block_num, 1), jnp.float32, 0.0, math.log(10.0)))
    return (base * row_scale * block_scale).reshape(HOURS, STATIONS, 2, BINS).astype(jnp.bfloat16)


def draw_src_ids(key, part):
    key_owner, key_order, key_shift, key_shuffle = jax.random.split(jax.random.fold_in(key, 23), 4)
    shard_count = STATIONS // STA_DEV
    owners = jax.random.randint(key_owner, (ROUNDS,), 0, shard_count)
    chosen = jax.random.permutation(key_order, ROUNDS)
    owners = owners.at[chosen[0]].set(0).at[chosen[1]].set(shard_count - 1)
    shifts = jax.random.randint(key_shift, (ROUNDS,), 0, STA_DEV)
    shifts = shifts.at[chosen[0]].set(0).at[chosen[1]].set(STA_DEV - 1)
    shuffles = jax.vmap(lambda one_key: jax.random.permutation(one_key, STA_DEV))(jax.random.split(key_shuffle, ROUNDS))
    offsets = jnp.remainder(shuffles - shuffles[:, :1] + shifts[:, None], STA_DEV)
    return (owners[:, None] * STA_DEV + offsets[:, :NSRC]).astype(jnp.int32)


def setup_inputs(seed: int = 0) -> dict:
    key_of = jax.random.split(jax.random.key(seed), 3)
    spectra = draw_spectra(jax.random.fold_in(key_of[2], 71), 0)
    src_ids = draw_src_ids(jax.random.fold_in(key_of[2], 71), 0)
    return dict(spectra=spectra, src_ids=src_ids)


EPSILON = 1e-05

def block_sums(spec):
    values = spec.astype(jnp.float32)
    magnitude = jnp.sqrt(values[..., 0, :] * values[..., 0, :] + values[..., 1, :] * values[..., 1, :])
    full_shape = magnitude.shape
    return magnitude.reshape(full_shape[:-1] + (full_shape[-1] // BLOCK, BLOCK)).sum(axis=-1)

def level_divide(spec, padded):
    block_num = padded.shape[-1] - 2
    level_mean = (padded[..., :-2] + padded[..., 1:-1] + padded[..., 2:]) / (3.0 * BLOCK)
    full_shape = spec.shape
    grid_view = spec.astype(jnp.float32).reshape(full_shape[:-1] + (block_num, BLOCK))
    whitened = grid_view / (level_mean[..., None, :, None] + EPSILON)
    return whitened.reshape(full_shape).astype(jnp.bfloat16)

def make_table(total_hours):
    lag_index = lax.iota(jnp.int32, LAGS) - LAGS // 2
    freq_index = lax.iota(jnp.int32, BINS)
    phase_int = jnp.remainder(lag_index[:, None] * freq_index[None, :], 2 * BINS)
    angle_rad = 2.0 * math.pi / (2 * BINS) * phase_int.astype(jnp.float32)
    norm_scale = 1.0 / math.sqrt(BINS * total_hours)
    return jnp.concatenate([jnp.cos(angle_rad) * norm_scale, -jnp.sin(angle_rad) * norm_scale], axis=1).astype(jnp.bfloat16)

def cross_block(sources, receivers):
    source_f = sources.astype(jnp.float32)
    receive_f = receivers.astype(jnp.float32)
    real_part = lax.optimization_barrier(jnp.sum(source_f[:, :, None, 0] * receive_f[:, None, :, 0] + source_f[:, :, None, 1] * receive_f[:, None, :, 1], axis=0))
    imag_part = lax.optimization_barrier(jnp.sum(source_f[:, :, None, 1] * receive_f[:, None, :, 0] - source_f[:, :, None, 0] * receive_f[:, None, :, 1], axis=0))
    count_src = sources.shape[1]
    count_rcv = receivers.shape[1]
    stacked = jnp.stack([real_part, imag_part], axis=2).astype(jnp.bfloat16)
    return stacked.reshape(count_src * count_rcv, 2 * sources.shape[-1])

def reference(spectra, src_ids):

    def whiten_hour(one_hour):
        totals = block_sums(one_hour)
        return level_divide(one_hour, jnp.pad(totals, ((0, 0), (1, 1))))
    whitened = lax.map(whiten_hour, spectra)
    transform = make_table(HOURS).astype(jnp.float32)
    group_count = HOURS // HR_DEV
    block_count = STATIONS // STA_DEV
    results = []
    for step_no in range(ROUNDS):
        sources = jnp.take(whitened, src_ids[step_no], axis=1)

        def one_block(position):
            receivers = lax.dynamic_slice_in_dim(whitened, position * STA_DEV, STA_DEV, 1)
            summed = jnp.zeros((LAGS, NSRC * STA_DEV), jnp.float32)
            for group_no in range(group_count):
                low = group_no * HR_DEV
                cross_spec = cross_block(sources[low:low + HR_DEV], receivers[low:low + HR_DEV])
                summed = summed + lax.dot_general(transform, cross_spec.astype(jnp.float32), (((1,), (1,)), ((), ())), precision=lax.Precision.HIGHEST)
            return summed.reshape(LAGS, NSRC, STA_DEV)
        stacked = lax.map(one_block, jnp.arange(block_count, dtype=jnp.int32))
        results.append(jnp.transpose(stacked, (1, 2, 0, 3)).reshape(LAGS, NSRC, STATIONS))
    return jnp.stack(results)
```

```python
import functools
import math

import jax
import jax.numpy as jnp
from jax import lax
from jax.experimental import pallas as pl
from jax.experimental.pallas import tpu as pltpu
from jax.sharding import PartitionSpec as P

BINS = 4096
BLOCK = 64
LAGS = 256
NSRC = 8
ROUNDS = 3
HR_DEV = 2
EPSILON = 1e-05
SPLIT = 2
COLS = 128


def make_table(chunk_num, total_hours):
    bins_chunk = BINS // chunk_num
    shape = (chunk_num, bins_chunk, LAGS)
    freq = lax.broadcasted_iota(jnp.int32, shape, 0) * bins_chunk + lax.broadcasted_iota(jnp.int32, shape, 1)
    lag = lax.broadcasted_iota(jnp.int32, shape, 2) - LAGS // 2
    phase = jnp.bitwise_and(lag * freq, 2 * BINS - 1)
    angle = 2.0 * math.pi / (2 * BINS) * phase.astype(jnp.float32)
    scale = 1.0 / math.sqrt(BINS * total_hours)
    return jnp.concatenate([jnp.cos(angle) * scale, -jnp.sin(angle) * scale], axis=1).astype(jnp.bfloat16)


def split3(value):
    high = value.astype(jnp.bfloat16)
    rest = value - high.astype(jnp.float32)
    middle = rest.astype(jnp.bfloat16)
    low = (rest - middle.astype(jnp.float32)).astype(jnp.bfloat16)
    return high, middle, low


def exact_dot(value, ones):
    return sum(jnp.dot(part, ones, preferred_element_type=jnp.float32) for part in split3(value))


def inverse_levels(src_ref, inv_ref):
    chunk_num, hours, _, rows, width = src_ref.shape
    for hour in range(hours):

        def add_chunk(chunk, total, hour=hour):
            real = src_ref[chunk, hour, 0].astype(jnp.float32)
            imag = src_ref[chunk, hour, 1].astype(jnp.float32)
            magnitude = jnp.minimum(jnp.sqrt(real * real + imag * imag), 2.0**127)
            block = (lax.broadcasted_iota(jnp.int32, (width, COLS), 0) + chunk * width) // BLOCK
            away = block - lax.broadcasted_iota(jnp.int32, (width, COLS), 1)
            near = jnp.where((away >= -1) & (away <= 1), 1.0, 0.0).astype(jnp.bfloat16)
            return total + exact_dot(magnitude, near)

        total = lax.fori_loop(0, chunk_num, add_chunk, jnp.zeros((rows, COLS), jnp.float32))
        inv_ref[hour] = 1.0 / (total / (3.0 * BLOCK) + EPSILON)


def expand(inv_ref, chunk, width, hour):
    block = (lax.broadcasted_iota(jnp.int32, (COLS, width), 1) + chunk * width) // BLOCK
    same = jnp.where(block == lax.broadcasted_iota(jnp.int32, (COLS, width), 0), 1.0, 0.0)
    return exact_dot(inv_ref[hour], same.astype(jnp.bfloat16))


def correlate_kernel(x_ref, y_ref, t_ref, o_ref, inv_x, inv_y, xw, yw, yb, cross_a, cross_b, total):
    chunk = pl.program_id(0)
    chunk_num, hours, _, rows, width = x_ref.shape
    sources = y_ref.shape[3]

    @pl.when(chunk == 0)
    def _():
        inverse_levels(x_ref, inv_x)
        inverse_levels(y_ref, inv_y)
        total[...] = jnp.zeros_like(total)

    for hour in range(hours):
        scale_x = expand(inv_x, chunk, width, hour)
        scale_y = expand(inv_y, chunk, width, hour)
        for part in range(2):
            xw[hour, part] = (x_ref[chunk, hour, part].astype(jnp.float32) * scale_x).astype(jnp.bfloat16)
            yw[hour * 2 + part] = y_ref[chunk, hour, part].astype(jnp.float32) * scale_y

    def spread_source(k, carry):
        for piece in range(2 * hours):
            row = yw[piece, pl.ds(k, 1), :]
            yb[k, piece] = jnp.broadcast_to(row, (16, width)).astype(jnp.bfloat16)
        return carry

    lax.fori_loop(0, sources, spread_source, 0)

    for step in range(ROUNDS):
        cross = (cross_a, cross_b)[step % 2]
        for k in range(NSRC):
            for low in range(0, width, 128):
                lanes = slice(low, low + 128)
                y = [yb[step * NSRC + k, piece, :, lanes][None] for piece in range(2 * hours)]
                x = [xw[piece // 2, piece % 2, :, lanes].reshape(rows // 16, 16, 128) for piece in range(2 * hours)]
                real = (y[0] * x[0] + y[1] * x[1]) + (y[2] * x[2] + y[3] * x[3])
                imag = (y[1] * x[0] - y[0] * x[1]) + (y[3] * x[2] - y[2] * x[3])
                cross[k * rows:(k + 1) * rows, lanes] = real.reshape(rows, 128)
                cross[k * rows:(k + 1) * rows, width + low:width + low + 128] = imag.reshape(rows, 128)
        total[step] += jnp.dot(cross[...], t_ref[0], preferred_element_type=jnp.float32)

    @pl.when(chunk == chunk_num - 1)
    def _():
        for step in range(ROUNDS):
            o_ref[:, step * NSRC * rows:(step + 1) * NSRC * rows] = total[step].T.astype(jnp.bfloat16)


def correlate(x, y, table):
    chunk_num, hours, _, rows, width = x.shape
    sources = y.shape[3]
    whole = lambda shape: pl.BlockSpec(shape, lambda i: (0,) * len(shape))
    return pl.pallas_call(
        correlate_kernel,
        grid=(chunk_num,),
        in_specs=[
            whole(x.shape),
            whole(y.shape),
            pl.BlockSpec((1, 2 * width, LAGS), lambda i: (i, 0, 0)),
        ],
        out_specs=whole((LAGS, sources * rows)),
        out_shape=jax.ShapeDtypeStruct((LAGS, sources * rows), jnp.bfloat16),
        scratch_shapes=[
            pltpu.VMEM((hours, rows, COLS), jnp.float32),
            pltpu.VMEM((hours, sources, COLS), jnp.float32),
            pltpu.VMEM((hours, 2, rows, width), jnp.bfloat16),
            pltpu.VMEM((2 * hours, sources, width), jnp.float32),
            pltpu.VMEM((sources, 2 * hours, 16, width), jnp.bfloat16),
            pltpu.VMEM((NSRC * rows, 2 * width), jnp.bfloat16),
            pltpu.VMEM((NSRC * rows, 2 * width), jnp.bfloat16),
            pltpu.VMEM((ROUNDS, NSRC * rows, LAGS), jnp.float32),
        ],
        compiler_params=pltpu.CompilerParams(
            dimension_semantics=("arbitrary",), vmem_limit_bytes=48 * 1024 * 1024
        ),
        cost_estimate=pl.CostEstimate(
            flops=2 * LAGS * sources * rows * 2 * BINS * 2, bytes_accessed=12 * 1024 * 1024, transcendentals=0
        ),
    )(x, y, table)


def local(spectra, src_ids):
    hours, stations, _, width = spectra.shape
    chunk_num = BINS // width
    tm = lax.axis_size("tm")
    dev_rows = stations // chunk_num
    rows = dev_rows // SPLIT
    picked = jnp.take(spectra, src_ids.reshape(-1), axis=1).transpose(0, 2, 1, 3)
    y = lax.all_gather(picked, "sta", axis=0, tiled=False)
    parted = spectra.reshape(hours, chunk_num, SPLIT, rows, 2, width).transpose(2, 1, 0, 4, 3, 5)
    table = make_table(chunk_num, hours * tm)
    results = []
    for half in range(SPLIT):
        x = lax.all_to_all(parted[half], "sta", split_axis=0, concat_axis=0, tiled=True)
        partial = correlate(x, y, table)
        stacked = lax.psum_scatter(partial, "tm", scatter_dimension=0, tiled=True)
        results.append(stacked.reshape(LAGS // tm, ROUNDS, NSRC, rows))
    joined = jnp.concatenate(results, axis=3).astype(jnp.float32)
    return joined.transpose(1, 0, 2, 3)


def solution(mesh):
    return jax.shard_map(
        local,
        mesh=mesh,
        in_specs=(P("tm", None, None, "sta"), P()),
        out_specs=P(None, "tm", None, "sta"),
        check_vma=False,
    )
```

```python
import functools
import math

import jax
import jax.numpy as jnp
from jax import lax
from jax.experimental import pallas as pl
from jax.experimental.pallas import tpu as pltpu
from jax.sharding import PartitionSpec as P

BINS = 4096
BLOCK = 64
LAGS = 256
NSRC = 8
ROUNDS = 3
HR_DEV = 2
EPSILON = 1e-05
SPLIT = 2
COLS = 128


def make_table(chunk_num, total_hours):
    bins_chunk = BINS // chunk_num
    shape = (chunk_num, bins_chunk, LAGS)
    freq = lax.broadcasted_iota(jnp.int32, shape, 0) * bins_chunk + lax.broadcasted_iota(jnp.int32, shape, 1)
    lag = lax.broadcasted_iota(jnp.int32, shape, 2) - LAGS // 2
    phase = jnp.bitwise_and(lag * freq, 2 * BINS - 1)
    angle = 2.0 * math.pi / (2 * BINS) * phase.astype(jnp.float32)
    scale = 1.0 / math.sqrt(BINS * total_hours)
    return (jnp.cos(angle) * scale).astype(jnp.bfloat16), (-jnp.sin(angle) * scale).astype(jnp.bfloat16)


def split_wide(value):
    high = value.astype(jnp.bfloat16)
    low = (value - high.astype(jnp.float32)).astype(jnp.bfloat16)
    return jnp.concatenate([high, low], axis=-1)


def twice(ones):
    ones = ones.astype(jnp.bfloat16)
    return jnp.concatenate([ones, ones], axis=0)


def inverse_levels(src_ref, inv_ref):
    chunk_num, hours, _, rows, width = src_ref.shape

    def add_chunk(chunk, total):
        terms = []
        for hour in range(hours):
            real = src_ref[chunk, hour, 0].astype(jnp.float32)
            imag = src_ref[chunk, hour, 1].astype(jnp.float32)
            terms.append(split_wide(jnp.minimum(jnp.sqrt(real * real + imag * imag), 2.0**127)))
        block = (lax.broadcasted_iota(jnp.int32, (width, COLS), 0) + chunk * width) // BLOCK
        away = block - lax.broadcasted_iota(jnp.int32, (width, COLS), 1)
        near = twice(jnp.where((away >= -1) & (away <= 1), 1.0, 0.0))
        return total + jnp.dot(jnp.concatenate(terms, axis=0), near, preferred_element_type=jnp.float32)

    total = lax.fori_loop(0, chunk_num, add_chunk, jnp.zeros((hours * rows, COLS), jnp.float32))
    inv_ref[...] = split_wide(1.0 / (total / (3.0 * BLOCK) + EPSILON))


def expand(inv_ref, chunk, width):
    block = (lax.broadcasted_iota(jnp.int32, (COLS, width), 1) + chunk * width) // BLOCK
    same = twice(jnp.where(block == lax.broadcasted_iota(jnp.int32, (COLS, width), 0), 1.0, 0.0))
    return jnp.dot(inv_ref[...], same, preferred_element_type=jnp.float32)


def sources_kernel(y_ref, o_ref, inv_y):
    chunk_num, hours, _, rows, width = y_ref.shape
    inverse_levels(y_ref, inv_y)

    def one_chunk(chunk, carry):
        scale = expand(inv_y, chunk, width)
        for hour in range(hours):
            for part in range(2):
                piece = y_ref[chunk, hour, part].astype(jnp.float32) * scale[hour * rows:(hour + 1) * rows]
                o_ref[chunk, hour * 2 + part] = piece.astype(jnp.bfloat16).astype(jnp.float32)
        return carry

    lax.fori_loop(0, chunk_num, one_chunk, 0)


def whiten_sources(y):
    chunk_num, hours, parts, sources, width = y.shape
    return pl.pallas_call(
        sources_kernel,
        in_specs=[pl.BlockSpec(memory_space=pltpu.VMEM)],
        out_specs=pl.BlockSpec(memory_space=pltpu.VMEM),
        out_shape=jax.ShapeDtypeStruct((chunk_num, hours * parts, sources, width), jnp.float32),
        scratch_shapes=[pltpu.VMEM((hours * sources, 2 * COLS), jnp.bfloat16)],
        compiler_params=pltpu.CompilerParams(vmem_limit_bytes=24 * 1024 * 1024),
        cost_estimate=pl.CostEstimate(flops=400 * 1000 * 1000, bytes_accessed=3 * 1024 * 1024, transcendentals=0),
    )(y)


def correlate_kernel(x_ref, y_ref, tr_ref, ti_ref, o_ref, inv_x, xw, real_a, imag_a, real_b, imag_b, total):
    chunk = pl.program_id(0)
    chunk_num, hours, _, rows, width = x_ref.shape

    @pl.when(chunk == 0)
    def _():
        inverse_levels(x_ref, inv_x)
        total[...] = jnp.zeros_like(total)

    scale = expand(inv_x, chunk, width)
    for hour in range(hours):
        for part in range(2):
            piece = x_ref[chunk, hour, part].astype(jnp.float32) * scale[hour * rows:(hour + 1) * rows]
            xw[hour * 2 + part] = piece.astype(jnp.bfloat16)

    for step in range(ROUNDS):
        real_ref, imag_ref = ((real_a, imag_a), (real_b, imag_b))[step % 2]
        for k in range(NSRC):
            for low in range(0, width, 128):
                lanes = slice(low, low + 128)
                row = step * NSRC + k
                y = [
                    jnp.broadcast_to(y_ref[0, piece, row:row + 1, lanes], (16, 128)).astype(jnp.bfloat16)[None]
                    for piece in range(2 * hours)
                ]
                x = [xw[piece, :, lanes].reshape(rows // 16, 16, 128) for piece in range(2 * hours)]
                real = (y[0] * x[0] + y[1] * x[1]) + (y[2] * x[2] + y[3] * x[3])
                imag = (y[1] * x[0] - y[0] * x[1]) + (y[3] * x[2] - y[2] * x[3])
                real_ref[k * rows:(k + 1) * rows, lanes] = real.reshape(rows, 128)
                imag_ref[k * rows:(k + 1) * rows, lanes] = imag.reshape(rows, 128)
        total[step] += jnp.dot(real_ref[...], tr_ref[0], preferred_element_type=jnp.float32) + jnp.dot(
            imag_ref[...], ti_ref[0], preferred_element_type=jnp.float32
        )

    @pl.when(chunk == chunk_num - 1)
    def _():
        for step in range(ROUNDS):
            o_ref[:, step * NSRC * rows:(step + 1) * NSRC * rows] = total[step].T.astype(jnp.bfloat16)


def correlate(x, y, table):
    chunk_num, hours, _, rows, width = x.shape
    sources = y.shape[2]
    whole = lambda shape: pl.BlockSpec(shape, lambda i: (0,) * len(shape))
    cross = pltpu.VMEM((NSRC * rows, width), jnp.bfloat16)
    return pl.pallas_call(
        correlate_kernel,
        grid=(chunk_num,),
        in_specs=[
            whole(x.shape),
            pl.BlockSpec((1,) + y.shape[1:], lambda i: (i, 0, 0, 0)),
            pl.BlockSpec((1, width, LAGS), lambda i: (i, 0, 0)),
            pl.BlockSpec((1, width, LAGS), lambda i: (i, 0, 0)),
        ],
        out_specs=whole((LAGS, sources * rows)),
        out_shape=jax.ShapeDtypeStruct((LAGS, sources * rows), jnp.bfloat16),
        scratch_shapes=[
            pltpu.VMEM((hours * rows, 2 * COLS), jnp.bfloat16),
            pltpu.VMEM((hours * 2, rows, width), jnp.bfloat16),
            cross,
            cross,
            cross,
            cross,
            pltpu.VMEM((ROUNDS, NSRC * rows, LAGS), jnp.float32),
        ],
        compiler_params=pltpu.CompilerParams(
            dimension_semantics=("arbitrary",), vmem_limit_bytes=40 * 1024 * 1024
        ),
        cost_estimate=pl.CostEstimate(
            flops=2 * LAGS * sources * rows * 2 * BINS * 2, bytes_accessed=12 * 1024 * 1024, transcendentals=0
        ),
    )(x, y, *table)


def local(spectra, src_ids):
    hours, stations, _, width = spectra.shape
    chunk_num = BINS // width
    tm = lax.axis_size("tm")
    rows = stations // chunk_num // SPLIT
    picked = jnp.take(spectra, src_ids.reshape(-1), axis=1, mode="clip").transpose(0, 2, 1, 3)
    copies = jnp.broadcast_to(picked[None], (chunk_num,) + picked.shape)
    y = whiten_sources(lax.all_to_all(copies, "sta", split_axis=0, concat_axis=0, tiled=True))
    parted = spectra.reshape(hours, chunk_num, SPLIT, rows, 2, width)
    table = make_table(chunk_num, hours * tm)
    results = []
    for half in range(SPLIT):
        leaving = parted[:, :, half].transpose(1, 0, 3, 2, 4)
        x = lax.all_to_all(leaving, "sta", split_axis=0, concat_axis=0, tiled=True)
        partial = correlate(x, y, table)
        stacked = lax.psum_scatter(partial, "tm", scatter_dimension=0, tiled=True)
        results.append(stacked.reshape(LAGS // tm, ROUNDS, NSRC, rows))
    joined = jnp.concatenate(results, axis=3).astype(jnp.float32)
    return joined.transpose(1, 0, 2, 3)


def solution(mesh):
    return jax.shard_map(
        local,
        mesh=mesh,
        in_specs=(P("tm", None, None, "sta"), P()),
        out_specs=P(None, "tm", None, "sta"),
        check_vma=False,
    )
```

```python
import functools
import math

import jax
import jax.numpy as jnp
from jax import lax
from jax.experimental import pallas as pl
from jax.experimental.pallas import tpu as pltpu
from jax.sharding import PartitionSpec as P

BINS = 4096
BLOCK = 64
LAGS = 256
NSRC = 8
ROUNDS = 3
HR_DEV = 2
EPSILON = 1e-05
PARTS = (3, 3, 2)
COLS = 128


def make_table(chunk_num, total_hours):
    bins_chunk = BINS // chunk_num
    shape = (chunk_num, bins_chunk, LAGS)
    freq = lax.broadcasted_iota(jnp.int32, shape, 0) * bins_chunk + lax.broadcasted_iota(jnp.int32, shape, 1)
    lag = lax.broadcasted_iota(jnp.int32, shape, 2) - LAGS // 2
    phase = jnp.bitwise_and(lag * freq, 2 * BINS - 1)
    angle = 2.0 * math.pi / (2 * BINS) * phase.astype(jnp.float32)
    scale = 1.0 / math.sqrt(BINS * total_hours)
    return (jnp.cos(angle) * scale).astype(jnp.bfloat16), (-jnp.sin(angle) * scale).astype(jnp.bfloat16)


def split_wide(value):
    high = value.astype(jnp.bfloat16)
    low = (value - high.astype(jnp.float32)).astype(jnp.bfloat16)
    return jnp.concatenate([high, low], axis=-1)


def twice(ones):
    ones = ones.astype(jnp.bfloat16)
    return jnp.concatenate([ones, ones], axis=0)


def inverse_levels(src_ref, inv_ref):
    chunk_num, hours, _, rows, width = src_ref.shape

    def add_chunk(chunk, total):
        terms = []
        for hour in range(hours):
            real = src_ref[chunk, hour, 0].astype(jnp.float32)
            imag = src_ref[chunk, hour, 1].astype(jnp.float32)
            terms.append(split_wide(jnp.minimum(jnp.sqrt(real * real + imag * imag), 2.0**127)))
        block = (lax.broadcasted_iota(jnp.int32, (width, COLS), 0) + chunk * width) // BLOCK
        away = block - lax.broadcasted_iota(jnp.int32, (width, COLS), 1)
        near = twice(jnp.where((away >= -1) & (away <= 1), 1.0, 0.0))
        return total + jnp.dot(jnp.concatenate(terms, axis=0), near, preferred_element_type=jnp.float32)

    total = lax.fori_loop(0, chunk_num, add_chunk, jnp.zeros((hours * rows, COLS), jnp.float32))
    inv_ref[...] = split_wide(1.0 / (total / (3.0 * BLOCK) + EPSILON))


def expand(inv_ref, chunk, width):
    block = (lax.broadcasted_iota(jnp.int32, (COLS, width), 1) + chunk * width) // BLOCK
    same = twice(jnp.where(block == lax.broadcasted_iota(jnp.int32, (COLS, width), 0), 1.0, 0.0))
    return jnp.dot(inv_ref[...], same, preferred_element_type=jnp.float32)


def sources_kernel(y_ref, o_ref, inv_y):
    chunk_num, hours, _, rows, width = y_ref.shape
    inverse_levels(y_ref, inv_y)

    def one_chunk(chunk, carry):
        scale = expand(inv_y, chunk, width)
        for hour in range(hours):
            for part in range(2):
                piece = y_ref[chunk, hour, part].astype(jnp.float32) * scale[hour * rows:(hour + 1) * rows]
                o_ref[chunk, hour * 2 + part] = piece.astype(jnp.bfloat16).astype(jnp.float32)
        return carry

    lax.fori_loop(0, chunk_num, one_chunk, 0)


def whiten_sources(y):
    chunk_num, hours, parts, sources, width = y.shape
    return pl.pallas_call(
        sources_kernel,
        in_specs=[pl.BlockSpec(memory_space=pltpu.VMEM)],
        out_specs=pl.BlockSpec(memory_space=pltpu.VMEM),
        out_shape=jax.ShapeDtypeStruct((chunk_num, hours * parts, sources, width), jnp.float32),
        scratch_shapes=[pltpu.VMEM((hours * sources, 2 * COLS), jnp.bfloat16)],
        compiler_params=pltpu.CompilerParams(vmem_limit_bytes=16 * 1024 * 1024),
        cost_estimate=pl.CostEstimate(flops=400 * 1000 * 1000, bytes_accessed=3 * 1024 * 1024, transcendentals=0),
    )(y)


def correlate_kernel(x_ref, y_ref, tr_ref, ti_ref, o_ref, inv_x, xw, real_a, imag_a, real_b, imag_b, total):
    chunk = pl.program_id(0)
    chunk_num, hours, _, rows, width = x_ref.shape

    @pl.when(chunk == 0)
    def _():
        inverse_levels(x_ref, inv_x)
        total[...] = jnp.zeros_like(total)

    scale = expand(inv_x, chunk, width)
    for hour in range(hours):
        for part in range(2):
            piece = x_ref[chunk, hour, part].astype(jnp.float32) * scale[hour * rows:(hour + 1) * rows]
            xw[hour * 2 + part] = piece.astype(jnp.bfloat16)

    for step in range(ROUNDS):
        real_ref, imag_ref = ((real_a, imag_a), (real_b, imag_b))[step % 2]
        for k in range(NSRC):
            for low in range(0, width, 128):
                lanes = slice(low, low + 128)
                row = step * NSRC + k
                y = [
                    jnp.broadcast_to(y_ref[0, piece, row:row + 1, lanes], (16, 128)).astype(jnp.bfloat16)[None]
                    for piece in range(2 * hours)
                ]
                x = [xw[piece, :, lanes].reshape(rows // 16, 16, 128) for piece in range(2 * hours)]
                real = (y[0] * x[0] + y[1] * x[1]) + (y[2] * x[2] + y[3] * x[3])
                imag = (y[1] * x[0] - y[0] * x[1]) + (y[3] * x[2] - y[2] * x[3])
                real_ref[k * rows:(k + 1) * rows, lanes] = real.reshape(rows, 128)
                imag_ref[k * rows:(k + 1) * rows, lanes] = imag.reshape(rows, 128)
        total[step] += jnp.dot(real_ref[...], tr_ref[0], preferred_element_type=jnp.float32) + jnp.dot(
            imag_ref[...], ti_ref[0], preferred_element_type=jnp.float32
        )

    @pl.when(chunk == chunk_num - 1)
    def _():
        for step in range(ROUNDS):
            o_ref[:, step * NSRC * rows:(step + 1) * NSRC * rows] = total[step].T.astype(jnp.bfloat16)


def correlate(x, y, table):
    chunk_num, hours, _, rows, width = x.shape
    sources = y.shape[2]
    whole = lambda shape: pl.BlockSpec(shape, lambda i: (0,) * len(shape))
    cross = pltpu.VMEM((NSRC * rows, width), jnp.bfloat16)
    return pl.pallas_call(
        correlate_kernel,
        grid=(chunk_num,),
        in_specs=[
            whole(x.shape),
            pl.BlockSpec((1,) + y.shape[1:], lambda i: (i, 0, 0, 0)),
            pl.BlockSpec((1, width, LAGS), lambda i: (i, 0, 0)),
            pl.BlockSpec((1, width, LAGS), lambda i: (i, 0, 0)),
        ],
        out_specs=whole((LAGS, sources * rows)),
        out_shape=jax.ShapeDtypeStruct((LAGS, sources * rows), jnp.bfloat16),
        scratch_shapes=[
            pltpu.VMEM((hours * rows, 2 * COLS), jnp.bfloat16),
            pltpu.VMEM((hours * 2, rows, width), jnp.bfloat16),
            cross,
            cross,
            cross,
            cross,
            pltpu.VMEM((ROUNDS, NSRC * rows, LAGS), jnp.float32),
        ],
        compiler_params=pltpu.CompilerParams(
            dimension_semantics=("arbitrary",), vmem_limit_bytes=24 * 1024 * 1024
        ),
        cost_estimate=pl.CostEstimate(
            flops=2 * LAGS * sources * rows * 2 * BINS * 2, bytes_accessed=12 * 1024 * 1024, transcendentals=0
        ),
    )(x, y, *table)


def local(spectra, src_ids):
    hours, stations, _, width = spectra.shape
    chunk_num = BINS // width
    tm = lax.axis_size("tm")
    dev_rows = stations // chunk_num
    picked = jnp.take(spectra, src_ids.reshape(-1), axis=1, mode="clip").transpose(0, 2, 1, 3)
    copies = jnp.broadcast_to(picked[None], (chunk_num,) + picked.shape)
    y = whiten_sources(lax.all_to_all(copies, "sta", split_axis=0, concat_axis=0, tiled=True))
    parted = spectra.reshape(hours, chunk_num, dev_rows, 2, width)
    table = make_table(chunk_num, hours * tm)
    arrived, results = [], []
    first = 0
    for number, share in enumerate(PARTS):
        rows = dev_rows * share // sum(PARTS)
        leaving = parted[:, :, first:first + rows].transpose(1, 0, 3, 2, 4)
        first += rows
        if number == 1:
            leaving, y, table = lax.optimization_barrier((leaving, y, table))
        arrived.append(lax.all_to_all(leaving, "sta", split_axis=0, concat_axis=0, tiled=True))
    for x in arrived:
        rows = x.shape[3]
        partial = correlate(x, y, table)
        stacked = lax.psum_scatter(partial, "tm", scatter_dimension=0, tiled=True)
        results.append(stacked.reshape(LAGS // tm, ROUNDS, NSRC, rows))
    joined = jnp.concatenate(results, axis=3).astype(jnp.float32)
    return joined.transpose(1, 0, 2, 3)


def solution(mesh):
    return jax.shard_map(
        local,
        mesh=mesh,
        in_specs=(P("tm", None, None, "sta"), P()),
        out_specs=P(None, "tm", None, "sta"),
        check_vma=False,
    )
```

```python
import functools
import math

import jax
import jax.numpy as jnp
from jax import lax
from jax.experimental import pallas as pl
from jax.experimental.pallas import tpu as pltpu
from jax.sharding import PartitionSpec as P

BINS = 4096
BLOCK = 64
LAGS = 256
NSRC = 8
ROUNDS = 3
HR_DEV = 2
EPSILON = 1e-05
PARTS = (1, 1)
COLS = 128


def make_table(chunk_num, total_hours):
    bins_chunk = BINS // chunk_num
    shape = (chunk_num, bins_chunk, LAGS)
    freq = lax.broadcasted_iota(jnp.int32, shape, 0) * bins_chunk + lax.broadcasted_iota(jnp.int32, shape, 1)
    lag = lax.broadcasted_iota(jnp.int32, shape, 2) - LAGS // 2
    phase = jnp.bitwise_and(lag * freq, 2 * BINS - 1)
    angle = 2.0 * math.pi / (2 * BINS) * phase.astype(jnp.float32)
    scale = 1.0 / math.sqrt(BINS * total_hours)
    return (jnp.cos(angle) * scale).astype(jnp.bfloat16), (-jnp.sin(angle) * scale).astype(jnp.bfloat16)


def split_wide(value):
    high = value.astype(jnp.bfloat16)
    low = (value - high.astype(jnp.float32)).astype(jnp.bfloat16)
    return jnp.concatenate([high, low], axis=-1)


def twice(ones):
    ones = ones.astype(jnp.bfloat16)
    return jnp.concatenate([ones, ones], axis=0)


def inverse_levels(src_ref, inv_ref):
    chunk_num, hours, _, rows, width = src_ref.shape

    def add_chunk(chunk, total):
        terms = []
        for hour in range(hours):
            real = src_ref[chunk, hour, 0].astype(jnp.float32)
            imag = src_ref[chunk, hour, 1].astype(jnp.float32)
            terms.append(split_wide(jnp.minimum(jnp.sqrt(real * real + imag * imag), 2.0**127)))
        block = (lax.broadcasted_iota(jnp.int32, (width, COLS), 0) + chunk * width) // BLOCK
        away = block - lax.broadcasted_iota(jnp.int32, (width, COLS), 1)
        near = twice(jnp.where((away >= -1) & (away <= 1), 1.0, 0.0))
        return total + jnp.dot(jnp.concatenate(terms, axis=0), near, preferred_element_type=jnp.float32)

    total = lax.fori_loop(0, chunk_num, add_chunk, jnp.zeros((hours * rows, COLS), jnp.float32))
    inv_ref[...] = split_wide(1.0 / (total / (3.0 * BLOCK) + EPSILON))


def expand(inv_ref, chunk, width):
    block = (lax.broadcasted_iota(jnp.int32, (COLS, width), 1) + chunk * width) // BLOCK
    same = twice(jnp.where(block == lax.broadcasted_iota(jnp.int32, (COLS, width), 0), 1.0, 0.0))
    return jnp.dot(inv_ref[...], same, preferred_element_type=jnp.float32)


def sources_kernel(y_ref, o_ref, inv_y):
    chunk_num, hours, _, rows, width = y_ref.shape
    inverse_levels(y_ref, inv_y)

    def one_chunk(chunk, carry):
        scale = expand(inv_y, chunk, width)
        for hour in range(hours):
            for part in range(2):
                piece = y_ref[chunk, hour, part].astype(jnp.float32) * scale[hour * rows:(hour + 1) * rows]
                o_ref[chunk, hour * 2 + part] = piece.astype(jnp.bfloat16).astype(jnp.float32)
        return carry

    lax.fori_loop(0, chunk_num, one_chunk, 0)


def whiten_sources(y):
    chunk_num, hours, parts, sources, width = y.shape
    return pl.pallas_call(
        sources_kernel,
        in_specs=[pl.BlockSpec(memory_space=pltpu.VMEM)],
        out_specs=pl.BlockSpec(memory_space=pltpu.VMEM),
        out_shape=jax.ShapeDtypeStruct((chunk_num, hours * parts, sources, width), jnp.float32),
        scratch_shapes=[pltpu.VMEM((hours * sources, 2 * COLS), jnp.bfloat16)],
        compiler_params=pltpu.CompilerParams(vmem_limit_bytes=16 * 1024 * 1024),
        cost_estimate=pl.CostEstimate(flops=400 * 1000 * 1000, bytes_accessed=3 * 1024 * 1024, transcendentals=0),
    )(y)


def correlate_kernel(x_ref, y_ref, tr_ref, ti_ref, o_ref, inv_x, xw, real_a, imag_a, real_b, imag_b, total):
    chunk = pl.program_id(0)
    chunk_num, hours, _, rows, width = x_ref.shape

    @pl.when(chunk == 0)
    def _():
        inverse_levels(x_ref, inv_x)
        total[...] = jnp.zeros_like(total)

    scale = expand(inv_x, chunk, width)
    for hour in range(hours):
        for part in range(2):
            piece = x_ref[chunk, hour, part].astype(jnp.float32) * scale[hour * rows:(hour + 1) * rows]
            xw[hour * 2 + part] = piece.astype(jnp.bfloat16)

    for step in range(ROUNDS):
        real_ref, imag_ref = ((real_a, imag_a), (real_b, imag_b))[step % 2]
        for k in range(NSRC):
            for low in range(0, width, 128):
                lanes = slice(low, low + 128)
                row = step * NSRC + k
                y = [
                    jnp.broadcast_to(y_ref[0, piece, row:row + 1, lanes], (16, 128)).astype(jnp.bfloat16)[None]
                    for piece in range(2 * hours)
                ]
                x = [xw[piece, :, lanes].reshape(rows // 16, 16, 128) for piece in range(2 * hours)]
                real = (y[0] * x[0] + y[1] * x[1]) + (y[2] * x[2] + y[3] * x[3])
                imag = (y[1] * x[0] - y[0] * x[1]) + (y[3] * x[2] - y[2] * x[3])
                real_ref[k * rows:(k + 1) * rows, lanes] = real.reshape(rows, 128)
                imag_ref[k * rows:(k + 1) * rows, lanes] = imag.reshape(rows, 128)
        total[step] += jnp.dot(real_ref[...], tr_ref[0], preferred_element_type=jnp.float32) + jnp.dot(
            imag_ref[...], ti_ref[0], preferred_element_type=jnp.float32
        )

    @pl.when(chunk == chunk_num - 1)
    def _():
        for step in range(ROUNDS):
            o_ref[:, step * NSRC * rows:(step + 1) * NSRC * rows] = total[step].T.astype(jnp.bfloat16)


def correlate(x, y, table):
    chunk_num, hours, _, rows, width = x.shape
    sources = y.shape[2]
    whole = lambda shape: pl.BlockSpec(shape, lambda i: (0,) * len(shape))
    cross = pltpu.VMEM((NSRC * rows, width), jnp.bfloat16)
    return pl.pallas_call(
        correlate_kernel,
        grid=(chunk_num,),
        in_specs=[
            whole(x.shape),
            pl.BlockSpec((1,) + y.shape[1:], lambda i: (i, 0, 0, 0)),
            pl.BlockSpec((1, width, LAGS), lambda i: (i, 0, 0)),
            pl.BlockSpec((1, width, LAGS), lambda i: (i, 0, 0)),
        ],
        out_specs=whole((LAGS, sources * rows)),
        out_shape=jax.ShapeDtypeStruct((LAGS, sources * rows), jnp.bfloat16),
        scratch_shapes=[
            pltpu.VMEM((hours * rows, 2 * COLS), jnp.bfloat16),
            pltpu.VMEM((hours * 2, rows, width), jnp.bfloat16),
            cross,
            cross,
            cross,
            cross,
            pltpu.VMEM((ROUNDS, NSRC * rows, LAGS), jnp.float32),
        ],
        compiler_params=pltpu.CompilerParams(
            dimension_semantics=("arbitrary",), vmem_limit_bytes=56 * 1024 * 1024
        ),
        cost_estimate=pl.CostEstimate(
            flops=2 * LAGS * sources * rows * 2 * BINS * 2, bytes_accessed=12 * 1024 * 1024, transcendentals=0
        ),
    )(x, y, *table)


def local(spectra, src_ids):
    hours, stations, _, width = spectra.shape
    chunk_num = BINS // width
    tm = lax.axis_size("tm")
    dev_rows = stations // chunk_num
    picked = jnp.take(spectra, src_ids.reshape(-1), axis=1, mode="clip").transpose(0, 2, 1, 3)
    copies = jnp.broadcast_to(picked[None], (chunk_num,) + picked.shape)
    y = whiten_sources(lax.all_to_all(copies, "sta", split_axis=0, concat_axis=0, tiled=True))
    parted = spectra.reshape(hours, chunk_num, dev_rows, 2, width)
    table = make_table(chunk_num, hours * tm)
    arrived, results = [], []
    first = 0
    for number, share in enumerate(PARTS):
        rows = dev_rows * share // sum(PARTS)
        leaving = parted[:, :, first:first + rows].transpose(1, 0, 3, 2, 4)
        first += rows
        if number == 1:
            leaving, arrived[0], y, table = lax.optimization_barrier((leaving, arrived[0], y, table))
        arrived.append(lax.all_to_all(leaving, "sta", split_axis=0, concat_axis=0, tiled=True))
    for x in arrived:
        rows = x.shape[3]
        partial = correlate(x, y, table)
        stacked = lax.psum_scatter(partial, "tm", scatter_dimension=0, tiled=True)
        results.append(stacked.reshape(LAGS // tm, ROUNDS, NSRC, rows))
    joined = jnp.concatenate(results, axis=3).astype(jnp.float32)
    return joined.transpose(1, 0, 2, 3)


def solution(mesh):
    return jax.shard_map(
        local,
        mesh=mesh,
        in_specs=(P("tm", None, None, "sta"), P()),
        out_specs=P(None, "tm", None, "sta"),
        check_vma=False,
    )
```

```python
import functools
import math

import jax
import jax.numpy as jnp
from jax import lax
from jax.experimental import pallas as pl
from jax.experimental.pallas import tpu as pltpu
from jax.sharding import PartitionSpec as P

BINS = 4096
BLOCK = 64
LAGS = 256
NSRC = 8
ROUNDS = 3
HR_DEV = 2
EPSILON = 1e-05
PARTS = (1, 1)
COLS = 128


def make_table(chunk_num, total_hours):
    bins_chunk = BINS // chunk_num
    shape = (chunk_num, bins_chunk, LAGS)
    freq = lax.broadcasted_iota(jnp.int32, shape, 0) * bins_chunk + lax.broadcasted_iota(jnp.int32, shape, 1)
    lag = lax.broadcasted_iota(jnp.int32, shape, 2) - LAGS // 2
    phase = jnp.bitwise_and(lag * freq, 2 * BINS - 1)
    angle = 2.0 * math.pi / (2 * BINS) * phase.astype(jnp.float32)
    scale = 1.0 / math.sqrt(BINS * total_hours)
    return (jnp.cos(angle) * scale).astype(jnp.bfloat16), (-jnp.sin(angle) * scale).astype(jnp.bfloat16)


def split_wide(value):
    high = value.astype(jnp.bfloat16)
    low = (value - high.astype(jnp.float32)).astype(jnp.bfloat16)
    return jnp.concatenate([high, low], axis=-1)


def twice(ones):
    ones = ones.astype(jnp.bfloat16)
    return jnp.concatenate([ones, ones], axis=0)


def inverse_levels(src_ref, inv_ref):
    chunk_num, hours, _, rows, width = src_ref.shape

    def add_chunk(chunk, total):
        terms = []
        for hour in range(hours):
            real = src_ref[chunk, hour, 0].astype(jnp.float32)
            imag = src_ref[chunk, hour, 1].astype(jnp.float32)
            terms.append(split_wide(jnp.minimum(jnp.sqrt(real * real + imag * imag), 2.0**127)))
        block = (lax.broadcasted_iota(jnp.int32, (width, COLS), 0) + chunk * width) // BLOCK
        away = block - lax.broadcasted_iota(jnp.int32, (width, COLS), 1)
        near = twice(jnp.where((away >= -1) & (away <= 1), 1.0, 0.0))
        return total + jnp.dot(jnp.concatenate(terms, axis=0), near, preferred_element_type=jnp.float32)

    total = lax.fori_loop(0, chunk_num, add_chunk, jnp.zeros((hours * rows, COLS), jnp.float32), unroll=4)
    inv_ref[...] = split_wide(1.0 / (total / (3.0 * BLOCK) + EPSILON))


def expand(inv_ref, chunk, width):
    block = (lax.broadcasted_iota(jnp.int32, (COLS, width), 1) + chunk * width) // BLOCK
    same = twice(jnp.where(block == lax.broadcasted_iota(jnp.int32, (COLS, width), 0), 1.0, 0.0))
    return jnp.dot(inv_ref[...], same, preferred_element_type=jnp.float32)


def sources_kernel(y_ref, o_ref, inv_y):
    chunk_num, hours, _, rows, width = y_ref.shape
    inverse_levels(y_ref, inv_y)

    def one_chunk(chunk, carry):
        scale = expand(inv_y, chunk, width)
        for hour in range(hours):
            for part in range(2):
                piece = y_ref[chunk, hour, part].astype(jnp.float32) * scale[hour * rows:(hour + 1) * rows]
                o_ref[chunk, hour * 2 + part] = piece.astype(jnp.bfloat16).astype(jnp.float32)
        return carry

    lax.fori_loop(0, chunk_num, one_chunk, 0)


def whiten_sources(y):
    chunk_num, hours, parts, sources, width = y.shape
    return pl.pallas_call(
        sources_kernel,
        in_specs=[pl.BlockSpec(memory_space=pltpu.VMEM)],
        out_specs=pl.BlockSpec(memory_space=pltpu.VMEM),
        out_shape=jax.ShapeDtypeStruct((chunk_num, hours * parts, sources, width), jnp.float32),
        scratch_shapes=[pltpu.VMEM((hours * sources, 2 * COLS), jnp.bfloat16)],
        compiler_params=pltpu.CompilerParams(vmem_limit_bytes=16 * 1024 * 1024),
        cost_estimate=pl.CostEstimate(flops=400 * 1000 * 1000, bytes_accessed=3 * 1024 * 1024, transcendentals=0),
    )(y)


def correlate_kernel(x_ref, y_ref, tr_ref, ti_ref, o_ref, inv_x, xw, *buffers):
    chunk = pl.program_id(0)
    chunk_num, hours, _, rows, width = x_ref.shape
    total = buffers[-1]
    crosses = [buffers[2 * step:2 * step + 2] for step in range(ROUNDS)]

    @pl.when(chunk == 0)
    def _():
        inverse_levels(x_ref, inv_x)
        total[...] = jnp.zeros_like(total)

    scale = expand(inv_x, chunk, width)
    for hour in range(hours):
        for part in range(2):
            piece = x_ref[chunk, hour, part].astype(jnp.float32) * scale[hour * rows:(hour + 1) * rows]
            xw[hour * 2 + part] = piece.astype(jnp.bfloat16)

    def project(step):
        real_ref, imag_ref = crosses[step]
        total[step] += jnp.dot(real_ref[...], tr_ref[0], preferred_element_type=jnp.float32) + jnp.dot(
            imag_ref[...], ti_ref[0], preferred_element_type=jnp.float32
        )

    for step in range(ROUNDS):
        real_ref, imag_ref = crosses[step]
        for k in range(NSRC):
            for low in range(0, width, 128):
                lanes = slice(low, low + 128)
                row = step * NSRC + k
                y = [
                    jnp.broadcast_to(y_ref[0, piece, row:row + 1, lanes], (16, 128)).astype(jnp.bfloat16)[None]
                    for piece in range(2 * hours)
                ]
                x = [xw[piece, :, lanes].reshape(rows // 16, 16, 128) for piece in range(2 * hours)]
                real = (y[0] * x[0] + y[1] * x[1]) + (y[2] * x[2] + y[3] * x[3])
                imag = (y[1] * x[0] - y[0] * x[1]) + (y[3] * x[2] - y[2] * x[3])
                real_ref[k * rows:(k + 1) * rows, lanes] = real.reshape(rows, 128)
                imag_ref[k * rows:(k + 1) * rows, lanes] = imag.reshape(rows, 128)
        if step:
            project(step - 1)
    project(ROUNDS - 1)

    @pl.when(chunk == chunk_num - 1)
    def _():
        for step in range(ROUNDS):
            o_ref[:, step * NSRC * rows:(step + 1) * NSRC * rows] = total[step].T.astype(jnp.bfloat16)


def correlate(x, y, table):
    chunk_num, hours, _, rows, width = x.shape
    sources = y.shape[2]
    whole = lambda shape: pl.BlockSpec(shape, lambda i: (0,) * len(shape))
    cross = pltpu.VMEM((NSRC * rows, width), jnp.bfloat16)
    return pl.pallas_call(
        correlate_kernel,
        grid=(chunk_num,),
        in_specs=[
            whole(x.shape),
            pl.BlockSpec((1,) + y.shape[1:], lambda i: (i, 0, 0, 0)),
            pl.BlockSpec((1, width, LAGS), lambda i: (i, 0, 0)),
            pl.BlockSpec((1, width, LAGS), lambda i: (i, 0, 0)),
        ],
        out_specs=whole((LAGS, sources * rows)),
        out_shape=jax.ShapeDtypeStruct((LAGS, sources * rows), jnp.bfloat16),
        scratch_shapes=[
            pltpu.VMEM((hours * rows, 2 * COLS), jnp.bfloat16),
            pltpu.VMEM((hours * 2, rows, width), jnp.bfloat16),
            *([cross] * (2 * ROUNDS)),
            pltpu.VMEM((ROUNDS, NSRC * rows, LAGS), jnp.float32),
        ],
        compiler_params=pltpu.CompilerParams(
            dimension_semantics=("arbitrary",), vmem_limit_bytes=56 * 1024 * 1024
        ),
        cost_estimate=pl.CostEstimate(
            flops=2 * LAGS * sources * rows * 2 * BINS * 2, bytes_accessed=12 * 1024 * 1024, transcendentals=0
        ),
    )(x, y, *table)


def local(spectra, src_ids):
    hours, stations, _, width = spectra.shape
    chunk_num = BINS // width
    tm = lax.axis_size("tm")
    dev_rows = stations // chunk_num
    picked = jnp.take(spectra, src_ids.reshape(-1), axis=1, mode="clip").transpose(0, 2, 1, 3)
    copies = jnp.broadcast_to(picked[None], (chunk_num,) + picked.shape)
    y = whiten_sources(lax.all_to_all(copies, "sta", split_axis=0, concat_axis=0, tiled=True))
    parted = spectra.reshape(hours, chunk_num, dev_rows, 2, width)
    table = make_table(chunk_num, hours * tm)
    arrived, results = [], []
    first = 0
    for number, share in enumerate(PARTS):
        rows = dev_rows * share // sum(PARTS)
        leaving = parted[:, :, first:first + rows].transpose(1, 0, 3, 2, 4)
        first += rows
        if number == 1:
            leaving, arrived[0], y, table = lax.optimization_barrier((leaving, arrived[0], y, table))
        arrived.append(lax.all_to_all(leaving, "sta", split_axis=0, concat_axis=0, tiled=True))
    for x in arrived:
        rows = x.shape[3]
        partial = correlate(x, y, table)
        stacked = lax.psum_scatter(partial, "tm", scatter_dimension=0, tiled=True)
        results.append(stacked.reshape(LAGS // tm, ROUNDS, NSRC, rows))
    joined = jnp.concatenate(results, axis=3).astype(jnp.float32)
    return joined.transpose(1, 0, 2, 3)


def solution(mesh):
    return jax.shard_map(
        local,
        mesh=mesh,
        in_specs=(P("tm", None, None, "sta"), P()),
        out_specs=P(None, "tm", None, "sta"),
        check_vma=False,
    )
```
